32 devices in a mesh: dp: 4 (over y, x), tm: 8 (over z, core).
Axes of the slice: x: 2, y: 2, z: 4, core: 2. Of those that a mesh axis runs over, the one named last changes fastest.
Arguments:
- clips: bfloat16 [4, 128, 512, 512], P('dp', 'tm'), may hold values from -6 to 6
- w_time: bfloat16 [3, 512, 512], P(None, 'dp'), may hold values from -0.15625 to 0.15625
- gain: float32 [512], replicated, may hold values from 0.1 to 1.9
- rate: float32 [512], replicated, may hold values from 0.000390625 to 0.0333333333
- keep: float32 [128], P('tm'), may hold values from 0.5 to 1
- latent_ids: int32 [128], P('tm'), may hold values from 0 to 15, as said below
- w_lat: bfloat16 [512, 16], replicated, may hold values from -0.25 to 0.25
Outputs:
- features: bfloat16 [4, 128, 512, 512], P('dp', 'tm')
- latents: float32 [4, 16, 16, 512], P('dp', 'tm')
The draws below stay inside these ranges and needn't reach their ends.
Inputs may be any that keep to these rules, and one draw needn't show every extreme that they name: latent_ids never falls as the frame grows; latent frame j begins at a frame from j * 8 - 7 to j * 8 (latent 0 at frame 0) and ends where the next begins; every latent frame gets 1 to 15 frames and the last exactly 15.
All inputs are finite; a program needn't handle non-finite values.
Results may differ from the reference program's by a relative error of at most 0.0025.
Values may be sent and summed in bfloat16 or wider, within the bound.
A program may use at most 192 MiB of HBM per device.

```python
import math
import jax
import jax.numpy as jnp
from jax import lax

C = 512
LATC = 16
KT = 3
STRIDE = 8
P_SIZE = 512
VIDEO_LENGTH = 128
CLIPS = 4
LAT = 16


def draw_rate(key, part):
    first, second, final_portion = jax.random.split(key, 3)
    order = jax.random.permutation(first, C)
    fast_count = C // 2
    edge_markers = jnp.zeros((C,), jnp.float32).at[order[:fast_count]].set(1.0)
    fast = jax.random.uniform(second, (C,), jnp.float32, 1.0 / 50.0, 1.0 / 30.0)
    slow = jnp.exp(jax.random.uniform(final_portion, (C,), jnp.float32, math.log(0.05 / VIDEO_LENGTH), math.log(1.0 / VIDEO_LENGTH)))
    return edge_markers * fast + (1.0 - edge_markers) * slow


def draw_keep(key, part):
    first, second, final_portion = jax.random.split(key, 3)
    initial_displacement = jax.random.uniform(first, (VIDEO_LENGTH,), jnp.float32, 0.97, 1.0)
    order = jax.random.permutation(second, VIDEO_LENGTH)
    edge_markers = jnp.zeros((VIDEO_LENGTH,), jnp.float32).at[order[:3]].set(1.0)
    group_images = jax.random.uniform(final_portion, (VIDEO_LENGTH,), jnp.float32, 0.5, 0.8)
    return edge_markers * group_images + (1.0 - edge_markers) * initial_displacement


def draw_latent_ids(key, part):
    offsets = jax.random.randint(jax.random.fold_in(key, 11), (LAT,), 0, STRIDE).astype(jnp.int32)
    offsets = offsets.at[0].set(0).at[LAT - 1].set(STRIDE - 1)
    segment_starts = jnp.arange(LAT, dtype=jnp.int32) * STRIDE - offsets
    frames = jnp.arange(VIDEO_LENGTH, dtype=jnp.int32)
    return jnp.sum((frames[:, None] >= segment_starts[None, 1:]).astype(jnp.int32), 1).astype(jnp.int32)


def level_of(own_key, dims, cuts, smallest, high):
    loudness, own = 1.0, jax.random.fold_in(own_key, 6)
    for axis_at, parts in cuts:
        steps = jnp.exp(jax.random.uniform(jax.random.fold_in(own, axis_at), (parts,), jnp.float32, smallest / len(cuts), high / len(cuts)))
        loudness = loudness * jnp.repeat(steps, dims[axis_at] // parts).reshape([-1 if axis == axis_at else 1 for axis in range(len(dims))])
    return loudness


def centred(own_key, dims, spread, reach, cuts=(), held_as=jnp.bfloat16):
    result = jax.random.normal(own_key, dims, jnp.float32) * spread
    if len(cuts) > 0:
        result = level_of(own_key, dims, cuts, -0.22, 0.18) * result
    return jnp.clip(result, min=-reach, max=reach).astype(held_as)


def setup_inputs(seed: int = 0) -> dict:
    key_list = jax.random.split(jax.random.key(seed), 8)
    clips = centred(key_list[0], (CLIPS, VIDEO_LENGTH, P_SIZE, C), 1.0, 6.0, ((0, 4), (1, 8)))
    w_time = centred(key_list[1], (KT, C, C), (KT * C) ** -0.5, 0.15625, ((1, 4),))
    gain = jnp.clip(1.0 + 0.18 * jax.random.normal(key_list[2], (C,), jnp.float32), 0.1, 1.9)
    rate = draw_rate(jax.random.fold_in(key_list[7], 71), 0)
    keep = draw_keep(jax.random.fold_in(key_list[7], 71), 0)
    latent_ids = draw_latent_ids(jax.random.fold_in(key_list[7], 71), 0)
    w_lat = centred(key_list[6], (C, LATC), C ** -0.5, 0.25)
    return dict(clips=clips, w_time=w_time, gain=gain, rate=rate, keep=keep, latent_ids=latent_ids, w_lat=w_lat)


def causal_conv(clip, w_time):
    padded = jnp.concatenate([jnp.zeros((KT - 1,) + clip.shape[1:], clip.dtype), clip], 0)
    total = jnp.zeros((VIDEO_LENGTH * P_SIZE, C), jnp.float32)
    for k in range(KT):
        part = padded[KT - 1 - k:KT - 1 - k + VIDEO_LENGTH].reshape(VIDEO_LENGTH * P_SIZE, C)
        total = total + jnp.dot(part, w_time[k], preferred_element_type=jnp.float32)
    return total.reshape(VIDEO_LENGTH, P_SIZE, C)

def reference(clips, w_time, gain, rate, keep, latent_ids, w_lat):
    decay = jnp.exp(-rate)
    inject = jnp.sqrt(-jnp.expm1(-2.0 * rate))
    retain = decay[None, :] * keep[:, None]
    onehot = (latent_ids[:, None] == jnp.arange(LAT, dtype=jnp.int32)[None, :]).astype(jnp.float32)
    counts = lax.optimization_barrier(jnp.sum(onehot, 0))

    def one_clip(clip):
        conv = causal_conv(clip, w_time)
        features = (clip.astype(jnp.float32) + jax.nn.silu(conv)).astype(jnp.bfloat16)
        values = features.astype(jnp.float32)
        normed = values * lax.rsqrt(lax.optimization_barrier(jnp.mean(values * values, -1, keepdims=True)) + 1e-06) * gain

        def step(state, inputs):
            kept, entry = inputs
            state = kept[None, :] * state + inject[None, :] * entry
            return (state, state)
        _, state = lax.scan(step, jnp.zeros((P_SIZE, C), jnp.float32), (retain, normed))
        state_b = state.astype(jnp.bfloat16)
        proj = jnp.dot(state_b.reshape(VIDEO_LENGTH * P_SIZE, C), w_lat, preferred_element_type=jnp.float32)
        proj = jnp.transpose(proj.reshape(VIDEO_LENGTH, P_SIZE, LATC), (0, 2, 1))
        sums = jnp.einsum('fj,flp->jlp', onehot, proj, precision=lax.Precision.HIGHEST)
        return (features, sums / counts[:, None, None])
    features, latents = lax.map(one_clip, clips)
    return (features, latents)
```

```python
import functools
import jax
import jax.numpy as jnp
from jax import lax
from jax.experimental import pallas as pl
from jax.experimental.pallas import tpu as pltpu
from jax.sharding import PartitionSpec as P

KT = 3
STRIDE = 8
NT = (((1,), (1,)), ((), ()))
HI = lax.Precision.HIGHEST


def build_maps(nframe, nlat, base, keep_row, ids_row, keep_own, ids_own, rate_col, gain_col, wl, out_ref):
    nall = keep_row.shape[1]
    ncol = wl.shape[1]
    width = ncol // nlat
    end = base + nframe - 1
    frame = lax.broadcasted_iota(jnp.int32, (8, nall), 1)
    later = frame > end
    logs = jnp.where(later, jnp.log(keep_row), 0.0)
    tri = (lax.broadcasted_iota(jnp.int32, (nall, nall), 0) <= lax.broadcasted_iota(jnp.int32, (nall, nall), 1)).astype(jnp.float32)
    cum = jnp.dot(logs, tri, precision=HI, preferred_element_type=jnp.float32)[:1]
    steps = (frame[:1] - end).astype(jnp.float32)
    power = jnp.where(later[:1], cum - rate_col * steps, -200.0)
    dec = jnp.exp(power)
    pooled = (lax.broadcasted_iota(jnp.int32, (ncol, nall), 0) // width == ids_row).astype(jnp.float32)
    entry = lax.dot_general(dec, pooled, NT, precision=HI, preferred_element_type=jnp.float32)
    counts = lax.dot_general(jnp.ones((8, nall), jnp.float32), pooled, NT, preferred_element_type=jnp.float32)[:1]
    inject = jnp.sqrt(1.0 - jnp.exp(-2.0 * rate_col))
    small = 2.0 * rate_col
    series = small * (1.0 - small * (0.5 - small * (1.0 / 6.0 - small * (1.0 / 24.0 - small * (1.0 / 120.0)))))
    inject = jnp.where(small < 0.125, jnp.sqrt(series), inject)
    weight = wl * (inject * gain_col) / counts
    decay = jnp.exp(-rate_col)
    column = lax.broadcasted_iota(jnp.int32, (1, ncol), 1) // width
    here = (column == ids_own(nframe - 1)).astype(jnp.float32)
    total = here + entry
    out_ref[nframe - 1] = (weight * total).astype(jnp.bfloat16)
    for g in range(nframe - 2, -1, -1):
        here = (column == ids_own(g)).astype(jnp.float32)
        total = here + (decay * keep_own(g + 1)) * total
        out_ref[g] = (weight * total).astype(jnp.bfloat16)


def maps_kernel(nlat, keep_own, ids_own, keep_row, ids_row, rate_col, gain_col, wl, out_ref):
    nframe = out_ref.shape[0]
    base = lax.axis_index("tm") * nframe
    build_maps(
        nframe, nlat, base, keep_row[...], ids_row[...],
        lambda g: keep_own[g], lambda g: ids_own[g],
        rate_col[...], gain_col[...], wl[...], out_ref,
    )


def main_kernel(rows, clips, prior, w, maps, features, acc, xbuf, sems):
    step = pl.program_id(0)
    nframe = clips.shape[0]
    npos = clips.shape[1]
    halo = KT - 1

    def load(slot):
        source = prior.at[slot] if slot < halo else clips.at[slot - halo]
        return pltpu.make_async_copy(source, xbuf.at[slot], sems.at[slot])

    @pl.when(step == 0)
    def _():
        for slot in range(nframe + halo):
            load(slot).start()
        for slot in range(halo):
            load(slot).wait()
        acc[...] = jnp.zeros_like(acc)

    pltpu.make_async_copy(clips.at[step], xbuf.at[step + halo], sems.at[step + halo]).wait()
    for at in range(0, npos, rows):
        span = slice(at, at + rows)
        own = xbuf[step + halo, span]
        lhs = jnp.concatenate([own] + [xbuf[step + halo - k, span] for k in range(1, KT)], axis=1)
        half = 0.5 * jnp.dot(lhs, w[...], preferred_element_type=jnp.float32)
        value = own.astype(jnp.float32) + (half * jnp.tanh(half) + half)
        rounded = value.astype(jnp.bfloat16)
        features[0, span] = rounded
        kept = rounded.astype(jnp.float32)
        scale = lax.rsqrt(jnp.mean(kept * kept, axis=-1, keepdims=True) + 1e-06)
        acc[span] += scale * jnp.dot(rounded, maps[0], preferred_element_type=jnp.float32)


def main_call(clips, prior, w, maps, rows=512):
    nframe, npos, nchan = clips.shape
    ncol = maps.shape[-1]
    halo = KT - 1
    return pl.pallas_call(
        functools.partial(main_kernel, rows),
        grid=(nframe,),
        out_shape=(
            jax.ShapeDtypeStruct((nframe, npos, nchan), jnp.bfloat16),
            jax.ShapeDtypeStruct((npos, ncol), jnp.float32),
        ),
        in_specs=[
            pl.BlockSpec(memory_space=pl.ANY),
            pl.BlockSpec(memory_space=pl.ANY),
            pl.BlockSpec(w.shape, lambda i: (0, 0)),
            pl.BlockSpec((1, nchan, ncol), lambda i: (i, 0, 0)),
        ],
        out_specs=(
            pl.BlockSpec((1, npos, nchan), lambda i: (i, 0, 0)),
            pl.BlockSpec((npos, ncol), lambda i: (0, 0)),
        ),
        scratch_shapes=[
            pltpu.VMEM((nframe + halo, npos, nchan), jnp.bfloat16),
            pltpu.SemaphoreType.DMA((nframe + halo,)),
        ],
        compiler_params=pltpu.CompilerParams(vmem_limit_bytes=48 * 1024 * 1024),
    )(clips, prior, w, maps)


def per_device(clips, w_time, gain, rate, keep, latent_ids, w_lat):
    nclip, nframe, npos, nchan = clips.shape
    ntm = lax.axis_size("tm")
    nlat = nframe * ntm // STRIDE
    latc = w_lat.shape[1]
    halo = KT - 1
    tail = clips[:, nframe - halo:]
    prior = lax.ppermute(tail, "tm", [(s, s + 1) for s in range(ntm - 1)])[0]
    w = lax.all_gather(w_time, "dp", axis=1, tiled=True).reshape(KT * nchan, nchan)
    keep_all = lax.all_gather(keep, "tm", tiled=True)
    ids_all = lax.all_gather(latent_ids, "tm", tiled=True)
    wl = jnp.tile(w_lat.astype(jnp.float32), (1, nlat))
    maps = pl.pallas_call(
        functools.partial(maps_kernel, nlat),
        out_shape=jax.ShapeDtypeStruct((nframe, nchan, nlat * latc), jnp.bfloat16),
        in_specs=[pl.BlockSpec(memory_space=pltpu.SMEM)] * 2 + [pl.BlockSpec(memory_space=pltpu.VMEM)] * 5,
        out_specs=pl.BlockSpec(memory_space=pltpu.VMEM),
        compiler_params=pltpu.CompilerParams(vmem_limit_bytes=60 * 1024 * 1024),
    )(keep, latent_ids, keep_all[None], ids_all[None], rate[:, None], gain[:, None], wl)
    features, acc = main_call(clips[0], prior, w, maps)
    share = acc.T.reshape(nlat, latc, npos)
    latents = lax.psum_scatter(share, "tm", scatter_dimension=0, tiled=True)
    return (features[None], latents[None])


def solution(mesh):
    return jax.shard_map(
        per_device,
        mesh=mesh,
        in_specs=(P("dp", "tm", None, None), P(None, "dp", None), P(), P(), P("tm"), P("tm"), P()),
        out_specs=(P("dp", "tm", None, None), P("dp", "tm", None, None)),
        check_vma=False,
    )
```

```python
import functools
import jax
import jax.numpy as jnp
from jax import lax
from jax.experimental import pallas as pl
from jax.experimental.pallas import tpu as pltpu
from jax.sharding import PartitionSpec as P

KT = 3
STRIDE = 8
NT = (((1,), (1,)), ((), ()))
HI = lax.Precision.HIGHEST


MESH = pl.DeviceIdType.MESH


def maps_of(nframe, nlat, base, keep_row, ids_row, keep_own, ids_own, rate_row, gain_row, w_lat, out_ref):
    nall = keep_row.shape[1]
    nchan, latc = w_lat.shape
    ncol = nlat * latc
    rate_col = jnp.broadcast_to(rate_row, (128, nchan)).T[:, :1]
    gain_col = jnp.broadcast_to(gain_row, (128, nchan)).T[:, :1]
    spread = lax.broadcasted_iota(jnp.int32, (latc, ncol), 1) % latc == lax.broadcasted_iota(jnp.int32, (latc, ncol), 0)
    wl = jnp.dot(w_lat, spread.astype(jnp.bfloat16), preferred_element_type=jnp.float32)
    end = base + nframe - 1
    frame = lax.broadcasted_iota(jnp.int32, (8, nall), 1)
    later = frame > end
    logs = jnp.where(later, jnp.log(keep_row), 0.0)
    tri = (lax.broadcasted_iota(jnp.int32, (nall, nall), 0) <= lax.broadcasted_iota(jnp.int32, (nall, nall), 1)).astype(jnp.float32)
    cum = jnp.dot(logs, tri, precision=HI, preferred_element_type=jnp.float32)[:1]
    steps = (frame[:1] - end).astype(jnp.float32)
    power = jnp.where(later[:1], cum - rate_col * steps, -200.0)
    dec = jnp.exp(power)
    pooled = (lax.broadcasted_iota(jnp.int32, (ncol, nall), 0) // latc == ids_row).astype(jnp.float32)
    entry = lax.dot_general(dec, pooled, NT, precision=HI, preferred_element_type=jnp.float32)
    counts = lax.dot_general(jnp.ones((8, nall), jnp.float32), pooled, NT, preferred_element_type=jnp.float32)[:1]
    inject = jnp.sqrt(1.0 - jnp.exp(-2.0 * rate_col))
    small = 2.0 * rate_col
    series = small * (1.0 - small * (0.5 - small * (1.0 / 6.0 - small * (1.0 / 24.0 - small * (1.0 / 120.0)))))
    inject = jnp.where(small < 0.125, jnp.sqrt(series), inject)
    weight = wl * (inject * gain_col) / counts
    decay = jnp.exp(-rate_col)
    column = lax.broadcasted_iota(jnp.int32, (1, ncol), 1) // latc
    here = (column == ids_own(nframe - 1)).astype(jnp.float32)
    total = here + entry
    out_ref[nframe - 1] = (weight * total).astype(jnp.bfloat16)
    for g in range(nframe - 2, -1, -1):
        here = (column == ids_own(g)).astype(jnp.float32)
        total = here + (decay * keep_own(g + 1)) * total
        out_ref[g] = (weight * total).astype(jnp.bfloat16)


def gather_kernel(ntm, nlat, clips, w_time, keep_s, ids_s, keep_v, ids_v, rate, gain, w_lat,
                  w_full, prior, maps, small, zeros, local_sem, sw, rw, st, rt, sk, rk):
    halo = KT - 1
    nframe = clips.shape[0]
    shard = w_time.shape[1]
    d, t = lax.axis_index("dp"), lax.axis_index("tm")
    c = lax.rem(t, 2)
    sister = t + 1 - 2 * c
    xd = d + 1 - 2 * lax.rem(d, 2)
    yd = lax.rem(d + 2, 4)
    part = shard // 4

    barrier = pltpu.get_barrier_semaphore()
    for k in range(1, ntm):
        pl.semaphore_signal(barrier, inc=1, device_id=(d, lax.rem(t + k, ntm)), device_id_type=MESH)
    for other in (xd, yd):
        pl.semaphore_signal(barrier, inc=1, device_id=(other, t), device_id_type=MESH)
    own_copy = pltpu.make_async_copy(w_time, w_full.at[:, pl.ds(d * shard, shard)], local_sem.at[0])
    own_copy.start()
    nall = small.shape[-1]
    place = lax.broadcasted_iota(jnp.int32, (nframe, nall), 1) == lax.broadcasted_iota(jnp.int32, (nframe, nall), 0) + t * nframe
    place = place.astype(jnp.float32)
    keep8 = jnp.broadcast_to(keep_v[...], (8, nframe))
    ids8 = jnp.broadcast_to(ids_v[...].astype(jnp.float32), (8, nframe))
    pick = lax.broadcasted_iota(jnp.int32, (8, nframe), 0) == 0
    both = jnp.where(pick, keep8, ids8)
    small[0] = jnp.dot(both, place, precision=HI, preferred_element_type=jnp.float32)
    pl.semaphore_wait(barrier, ntm + 1)

    def rows(dev, core, q):
        return pl.ds(dev * shard + core * (2 * part) + q * part, part)

    def send(source, dest, index, device):
        return pltpu.make_async_remote_copy(
            src_ref=source, dst_ref=dest, send_sem=sw.at[index], recv_sem=rw.at[index],
            device_id=device, device_id_type=MESH)

    own = {}
    for q in range(2):
        source = w_time.at[:, pl.ds(c * (2 * part) + q * part, part)]
        dest = w_full.at[:, rows(d, c, q)]
        own[q] = send(source, dest, q, (xd, t))
        own[2 + q] = send(source, dest, 2 + q, (yd, t))
        own[q].start()
        own[2 + q].start()
    tail = pltpu.make_async_remote_copy(
        src_ref=clips.at[pl.ds(nframe - halo, halo)], dst_ref=prior, send_sem=st, recv_sem=rt,
        device_id=(d, lax.rem(t + 1, ntm)), device_id_type=MESH)

    @pl.when(t < ntm - 1)
    def _():
        tail.start()

    smalls = []
    for k in range(1, ntm):
        copy = pltpu.make_async_remote_copy(
            src_ref=small.at[0], dst_ref=small.at[k], send_sem=sk.at[k - 1], recv_sem=rk.at[k - 1],
            device_id=(d, lax.rem(t + k, ntm)), device_id_type=MESH)
        copy.start()
        smalls.append(copy)

    @pl.when(t == 0)
    def _():
        zeros[...] = jnp.zeros_like(zeros)
        for h in range(halo):
            fill = pltpu.make_async_copy(zeros, prior.at[h], local_sem.at[1])
            fill.start()
            fill.wait()

    for copy in smalls:
        copy.wait_recv()
    table = small[0]
    for k in range(1, ntm):
        table = table + small[k]

    diag = 3 - d
    got = {}
    def forward(dev, q, index, device):
        piece = w_full.at[:, rows(dev, c, q)]
        copy = send(piece, piece, index, device)
        copy.start()
        got[index] = copy

    own[0].wait_recv()
    forward(xd, 0, 4, (yd, t))
    forward(xd, 0, 6, (d, sister))
    own[3].wait_recv()
    forward(yd, 1, 5, (xd, t))
    forward(yd, 1, 9, (d, sister))
    own[1].wait_recv()
    forward(xd, 1, 7, (d, sister))
    own[2].wait_recv()
    forward(yd, 0, 8, (d, sister))

    maps_of(nframe, nlat, t * nframe, table[0:1], table[1:2].astype(jnp.int32),
            lambda g: keep_s[g], lambda g: ids_s[g], rate[...], gain[...], w_lat[...], maps)

    got[4].wait_recv()
    forward(diag, 0, 10, (d, sister))
    got[5].wait_recv()
    forward(diag, 1, 11, (d, sister))
    for index in range(6, 12):
        got[index].wait_recv()
    for index in range(4):
        own[index].wait_send()
    for index in range(4, 12):
        got[index].wait_send()
    for copy in smalls:
        copy.wait_send()
    own_copy.wait()

    @pl.when(t < ntm - 1)
    def _():
        tail.wait_send()

    @pl.when(t > 0)
    def _():
        tail.wait_recv()


def gather_call(clips, w_time, gain, rate, keep, ids, w_lat):
    nframe, npos, nchan = clips.shape
    ntm = lax.axis_size("tm")
    nall = nframe * ntm
    nlat = nall // STRIDE
    ncol = nlat * w_lat.shape[1]
    any_spec = pl.BlockSpec(memory_space=pl.ANY)
    smem = pl.BlockSpec(memory_space=pltpu.SMEM)
    vmem = pl.BlockSpec(memory_space=pltpu.VMEM)
    return pl.pallas_call(
        functools.partial(gather_kernel, ntm, nlat),
        out_shape=(
            jax.ShapeDtypeStruct((KT, nchan, nchan), jnp.bfloat16),
            jax.ShapeDtypeStruct((KT - 1, npos, nchan), jnp.bfloat16),
            jax.ShapeDtypeStruct((nframe, nchan, ncol), jnp.bfloat16),
        ),
        in_specs=[any_spec, any_spec, smem, smem] + [vmem] * 5,
        out_specs=(any_spec, any_spec, vmem),
        scratch_shapes=[
            pltpu.VMEM((ntm, 8, nall), jnp.float32),
            pltpu.VMEM((npos, nchan), jnp.bfloat16),
            pltpu.SemaphoreType.DMA((2,)),
            pltpu.SemaphoreType.DMA((12,)),
            pltpu.SemaphoreType.DMA((12,)),
            pltpu.SemaphoreType.DMA,
            pltpu.SemaphoreType.DMA,
            pltpu.SemaphoreType.DMA((ntm - 1,)),
            pltpu.SemaphoreType.DMA((ntm - 1,)),
        ],
        compiler_params=pltpu.CompilerParams(
            collective_id=0, has_side_effects=True, vmem_limit_bytes=60 * 1024 * 1024),
    )(clips, w_time, keep, ids, keep[None], ids[None], rate[None], gain[None], w_lat)


def main_kernel(rows, clips, prior, w, maps, features, acc, xbuf, sems):
    step = pl.program_id(0)
    nframe = clips.shape[0]
    npos = clips.shape[1]
    halo = KT - 1

    def load(slot):
        source = prior.at[slot] if slot < halo else clips.at[slot - halo]
        return pltpu.make_async_copy(source, xbuf.at[slot], sems.at[slot])

    @pl.when(step == 0)
    def _():
        for slot in range(nframe + halo):
            load(slot).start()
        for slot in range(halo):
            load(slot).wait()
        acc[...] = jnp.zeros_like(acc)

    pltpu.make_async_copy(clips.at[step], xbuf.at[step + halo], sems.at[step + halo]).wait()
    for at in range(0, npos, rows):
        span = slice(at, at + rows)
        own = xbuf[step + halo, span]
        lhs = jnp.concatenate([own] + [xbuf[step + halo - k, span] for k in range(1, KT)], axis=1)
        half = 0.5 * jnp.dot(lhs, w[...], preferred_element_type=jnp.float32)
        value = own.astype(jnp.float32) + (half * jnp.tanh(half) + half)
        rounded = value.astype(jnp.bfloat16)
        features[0, span] = rounded
        kept = rounded.astype(jnp.float32)
        scale = lax.rsqrt(jnp.mean(kept * kept, axis=-1, keepdims=True) + 1e-06)
        acc[span] += scale * jnp.dot(rounded, maps[0], preferred_element_type=jnp.float32)


def main_call(clips, prior, w, maps, rows=512):
    nframe, npos, nchan = clips.shape
    ncol = maps.shape[-1]
    halo = KT - 1
    return pl.pallas_call(
        functools.partial(main_kernel, rows),
        grid=(nframe,),
        out_shape=(
            jax.ShapeDtypeStruct((nframe, npos, nchan), jnp.bfloat16),
            jax.ShapeDtypeStruct((npos, ncol), jnp.float32),
        ),
        in_specs=[
            pl.BlockSpec(memory_space=pl.ANY),
            pl.BlockSpec(memory_space=pl.ANY),
            pl.BlockSpec(w.shape, lambda i: (0, 0)),
            pl.BlockSpec((1, nchan, ncol), lambda i: (i, 0, 0)),
        ],
        out_specs=(
            pl.BlockSpec((1, npos, nchan), lambda i: (i, 0, 0)),
            pl.BlockSpec((npos, ncol), lambda i: (0, 0)),
        ),
        scratch_shapes=[
            pltpu.VMEM((nframe + halo, npos, nchan), jnp.bfloat16),
            pltpu.SemaphoreType.DMA((nframe + halo,)),
        ],
        compiler_params=pltpu.CompilerParams(vmem_limit_bytes=48 * 1024 * 1024),
    )(clips, prior, w, maps)


def reduce_kernel(nchip, per, acc, out, mine, theirs, sums, slots, s1, r1, s2, r2):
    d, t = lax.axis_index("dp"), lax.axis_index("tm")
    c = lax.rem(t, 2)
    z = lax.div(t, 2)
    sister = t + 1 - 2 * c
    barrier = pltpu.get_barrier_semaphore()
    pl.semaphore_signal(barrier, inc=1, device_id=(d, sister), device_id_type=MESH)
    for k in range(1, nchip):
        pl.semaphore_signal(barrier, inc=1, device_id=(d, lax.rem(z + k, nchip) * 2 + c), device_id_type=MESH)
    turned = acc[...].T
    for e in range(2 * nchip):
        mine[e % 2, e // 2] = turned[e * per:(e + 1) * per]
    pl.semaphore_wait(barrier, nchip)
    swap = pltpu.make_async_remote_copy(
        src_ref=mine.at[1 - c], dst_ref=theirs, send_sem=s1, recv_sem=r1,
        device_id=(d, sister), device_id_type=MESH)
    swap.start()
    swap.wait_recv()
    sums[...] = (mine[c] + theirs[...]).astype(jnp.bfloat16)

    def copy(k):
        ahead = lax.rem(z + k, nchip)
        return pltpu.make_async_remote_copy(
            src_ref=sums.at[ahead], dst_ref=slots.at[k - 1], send_sem=s2.at[k - 1], recv_sem=r2.at[k - 1],
            device_id=(d, ahead * 2 + c), device_id_type=MESH)

    for k in range(nchip - 1, 0, -1):
        @pl.when(z + k < nchip)
        def _():
            copy(k).start()
    out[...] = mine[c, z] + theirs[z]
    for k in range(1, nchip):
        @pl.when(z >= k)
        def _():
            copy(k).wait_recv()
            out[...] += slots[k - 1].astype(jnp.float32)
    for k in range(1, nchip):
        @pl.when(z + k < nchip)
        def _():
            copy(k).wait_send()
    swap.wait_send()


def reduce_call(acc, per):
    npos, ncol = acc.shape
    nchip = lax.axis_size("tm") // 2
    vmem = pl.BlockSpec(memory_space=pltpu.VMEM)
    return pl.pallas_call(
        functools.partial(reduce_kernel, nchip, per),
        out_shape=jax.ShapeDtypeStruct((per, npos), jnp.float32),
        in_specs=[vmem],
        out_specs=vmem,
        scratch_shapes=[
            pltpu.VMEM((2, nchip, per, npos), jnp.float32),
            pltpu.VMEM((nchip, per, npos), jnp.float32),
            pltpu.VMEM((nchip, per, npos), jnp.bfloat16),
            pltpu.VMEM((nchip - 1, per, npos), jnp.bfloat16),
            pltpu.SemaphoreType.DMA,
            pltpu.SemaphoreType.DMA,
            pltpu.SemaphoreType.DMA((nchip - 1,)),
            pltpu.SemaphoreType.DMA((nchip - 1,)),
        ],
        compiler_params=pltpu.CompilerParams(
            collective_id=1, has_side_effects=True, vmem_limit_bytes=48 * 1024 * 1024),
    )(acc)


def per_device(clips, w_time, gain, rate, keep, latent_ids, w_lat):
    nclip, nframe, npos, nchan = clips.shape
    nown = nframe // STRIDE
    latc = w_lat.shape[1]
    w, prior, maps = gather_call(clips[0], w_time, gain, rate, keep, latent_ids, w_lat)
    features, acc = main_call(clips[0], prior, w.reshape(KT * nchan, nchan), maps)
    latents = reduce_call(acc, nown * latc).reshape(nown, latc, npos)
    return (features[None], latents[None])


def solution(mesh):
    return jax.shard_map(
        per_device,
        mesh=mesh,
        in_specs=(P("dp", "tm", None, None), P(None, "dp", None), P(), P(), P("tm"), P("tm"), P()),
        out_specs=(P("dp", "tm", None, None), P("dp", "tm", None, None)),
        check_vma=False,
    )
```

```python
import functools
import jax
import jax.numpy as jnp
from jax import lax
from jax.experimental import pallas as pl
from jax.experimental.pallas import tpu as pltpu
from jax.sharding import PartitionSpec as P

KT = 3
STRIDE = 8
NT = (((1,), (1,)), ((), ()))
HI = lax.Precision.HIGHEST


MESH = pl.DeviceIdType.MESH


def maps_of(nframe, nlat, base, keep_row, ids_row, keep_own, ids_own, rate_row, gain_row, w_lat, maps_ref):
    nall = keep_row.shape[1]
    latc, nchan = w_lat.shape
    ncol = nlat * latc
    rate_col = jnp.broadcast_to(rate_row, (128, nchan)).T[:, :1]
    gain_col = jnp.broadcast_to(gain_row, (128, nchan)).T[:, :1]
    spread = lax.broadcasted_iota(jnp.int32, (latc, ncol), 1) % latc == lax.broadcasted_iota(jnp.int32, (latc, ncol), 0)
    wl = lax.dot_general(w_lat, spread.astype(jnp.bfloat16), (((0,), (0,)), ((), ())), preferred_element_type=jnp.float32)
    end = base + nframe - 1
    frame = lax.broadcasted_iota(jnp.int32, (8, nall), 1)
    later = frame > end
    logs = jnp.where(later, jnp.log(keep_row), 0.0)
    tri = (lax.broadcasted_iota(jnp.int32, (nall, nall), 0) <= lax.broadcasted_iota(jnp.int32, (nall, nall), 1)).astype(jnp.float32)
    cum = jnp.dot(logs, tri, precision=HI, preferred_element_type=jnp.float32)[:1]
    steps = (frame[:1] - end).astype(jnp.float32)
    power = jnp.where(later[:1], cum - rate_col * steps, -200.0)
    dec = jnp.exp(power)
    pooled = (lax.broadcasted_iota(jnp.int32, (ncol, nall), 0) // latc == ids_row).astype(jnp.float32)
    entry = lax.dot_general(dec, pooled, NT, precision=HI, preferred_element_type=jnp.float32)
    counts = lax.dot_general(jnp.ones((8, nall), jnp.float32), pooled, NT, preferred_element_type=jnp.float32)[:1]
    inject = jnp.sqrt(1.0 - jnp.exp(-2.0 * rate_col))
    small = 2.0 * rate_col
    series = small * (1.0 - small * (0.5 - small * (1.0 / 6.0 - small * (1.0 / 24.0 - small * (1.0 / 120.0)))))
    inject = jnp.where(small < 0.125, jnp.sqrt(series), inject)
    weight = wl * (inject * gain_col) / counts
    decay = jnp.exp(-rate_col)
    column = lax.broadcasted_iota(jnp.int32, (1, ncol), 1) // latc
    here = [(column == ids_own(g)).astype(jnp.float32) for g in range(nframe)]
    yield
    chunk = nchan // 4
    for at in range(0, nchan, chunk):
        span = slice(at, at + chunk)
        scale, fade = weight[span], decay[span]
        total = here[nframe - 1] + entry[span]
        maps_ref[nframe - 1, span] = (scale * total).astype(jnp.bfloat16)
        for g in range(nframe - 2, -1, -1):
            total = here[g] + (fade * keep_own(g + 1)) * total
            maps_ref[g, span] = (scale * total).astype(jnp.bfloat16)
        yield


def gather_kernel(ntm, nlat, clips, w_time, keep_s, ids_s, keep_v, ids_v, rate, gain, w_lat,
                  w_full, prior, maps, small, zeros, local_sem, sw, rw, st, rt, sk, rk):
    halo = KT - 1
    nframe = clips.shape[0]
    shard = w_time.shape[1]
    d, t = lax.axis_index("dp"), lax.axis_index("tm")
    c = lax.rem(t, 2)
    sister = t + 1 - 2 * c
    xd = d + 1 - 2 * lax.rem(d, 2)
    yd = lax.rem(d + 2, 4)
    part = shard // 4

    barrier = pltpu.get_barrier_semaphore()
    for k in range(1, ntm):
        pl.semaphore_signal(barrier, inc=1, device_id=(d, lax.rem(t + k, ntm)), device_id_type=MESH)
    for other in (xd, yd):
        pl.semaphore_signal(barrier, inc=1, device_id=(other, t), device_id_type=MESH)
    own_copy = pltpu.make_async_copy(w_time, w_full.at[:, pl.ds(d * shard, shard)], local_sem.at[0])
    own_copy.start()
    nall = small.shape[-1]
    place = lax.broadcasted_iota(jnp.int32, (nframe, nall), 1) == lax.broadcasted_iota(jnp.int32, (nframe, nall), 0) + t * nframe
    place = place.astype(jnp.float32)
    keep8 = jnp.broadcast_to(keep_v[...], (8, nframe))
    ids8 = jnp.broadcast_to(ids_v[...].astype(jnp.float32), (8, nframe))
    pick = lax.broadcasted_iota(jnp.int32, (8, nframe), 0) == 0
    both = jnp.where(pick, keep8, ids8)
    small[0] = jnp.dot(both, place, precision=HI, preferred_element_type=jnp.float32)
    pl.semaphore_wait(barrier, ntm + 1)

    def rows(dev, core, q):
        return pl.ds(dev * shard + core * (2 * part) + q * part, part)

    def send(source, dest, index, device):
        return pltpu.make_async_remote_copy(
            src_ref=source, dst_ref=dest, send_sem=sw.at[index], recv_sem=rw.at[index],
            device_id=device, device_id_type=MESH)

    smalls = []
    for k in range(1, ntm):
        copy = pltpu.make_async_remote_copy(
            src_ref=small.at[0], dst_ref=small.at[k], send_sem=sk.at[k - 1], recv_sem=rk.at[k - 1],
            device_id=(d, lax.rem(t + k, ntm)), device_id_type=MESH)
        copy.start()
        smalls.append(copy)

    own = {}
    for q in range(2):
        source = w_time.at[:, pl.ds(c * (2 * part) + q * part, part)]
        dest = w_full.at[:, rows(d, c, q)]
        own[q] = send(source, dest, q, (xd, t))
        own[2 + q] = send(source, dest, 2 + q, (yd, t))
    for index in (0, 3, 1, 2):
        own[index].start()
    tail = pltpu.make_async_remote_copy(
        src_ref=clips.at[pl.ds(nframe - halo, halo)], dst_ref=prior, send_sem=st, recv_sem=rt,
        device_id=(d, lax.rem(t + 1, ntm)), device_id_type=MESH)

    @pl.when(t < ntm - 1)
    def _():
        tail.start()

    @pl.when(t == 0)
    def _():
        zeros[...] = jnp.zeros_like(zeros)
        for h in range(halo):
            fill = pltpu.make_async_copy(zeros, prior.at[h], local_sem.at[1])
            fill.start()
            fill.wait()

    for copy in smalls:
        copy.wait_recv()
    table = small[0]
    for k in range(1, ntm):
        table = table + small[k]

    diag = 3 - d
    got = {}
    def forward(dev, q, index, device):
        piece = w_full.at[:, rows(dev, c, q)]
        copy = send(piece, piece, index, device)
        copy.start()
        got[index] = copy

    making = maps_of(nframe, nlat, t * nframe, table[0:1], table[1:2].astype(jnp.int32),
                     lambda g: keep_s[g], lambda g: ids_s[g], rate[...], gain[...], w_lat[...], maps)
    next(making)
    own[0].wait_recv()
    forward(xd, 0, 4, (yd, t))
    forward(xd, 0, 6, (d, sister))
    own[3].wait_recv()
    forward(yd, 1, 5, (xd, t))
    forward(yd, 1, 9, (d, sister))
    next(making)
    own[1].wait_recv()
    forward(xd, 1, 7, (d, sister))
    own[2].wait_recv()
    forward(yd, 0, 8, (d, sister))
    next(making)
    next(making)
    got[4].wait_recv()
    forward(diag, 0, 10, (d, sister))
    got[5].wait_recv()
    forward(diag, 1, 11, (d, sister))
    next(making)
    for index in range(6, 12):
        got[index].wait_recv()
    for index in range(4):
        own[index].wait_send()
    for index in range(4, 12):
        got[index].wait_send()
    for copy in smalls:
        copy.wait_send()
    own_copy.wait()

    @pl.when(t < ntm - 1)
    def _():
        tail.wait_send()

    @pl.when(t > 0)
    def _():
        tail.wait_recv()


def gather_call(clips, w_time, gain, rate, keep, ids, w_lat):
    nframe, npos, nchan = clips.shape
    ntm = lax.axis_size("tm")
    nall = nframe * ntm
    nlat = nall // STRIDE
    ncol = nlat * w_lat.shape[1]
    any_spec = pl.BlockSpec(memory_space=pl.ANY)
    smem = pl.BlockSpec(memory_space=pltpu.SMEM)
    vmem = pl.BlockSpec(memory_space=pltpu.VMEM)
    return pl.pallas_call(
        functools.partial(gather_kernel, ntm, nlat),
        out_shape=(
            jax.ShapeDtypeStruct((KT, nchan, nchan), jnp.bfloat16),
            jax.ShapeDtypeStruct((KT - 1, npos, nchan), jnp.bfloat16),
            jax.ShapeDtypeStruct((nframe, nchan, ncol), jnp.bfloat16),
        ),
        in_specs=[any_spec, any_spec, smem, smem] + [vmem] * 5,
        out_specs=(any_spec, any_spec, vmem),
        scratch_shapes=[
            pltpu.VMEM((ntm, 8, nall), jnp.float32),
            pltpu.VMEM((npos, nchan), jnp.bfloat16),
            pltpu.SemaphoreType.DMA((2,)),
            pltpu.SemaphoreType.DMA((12,)),
            pltpu.SemaphoreType.DMA((12,)),
            pltpu.SemaphoreType.DMA,
            pltpu.SemaphoreType.DMA,
            pltpu.SemaphoreType.DMA((ntm - 1,)),
            pltpu.SemaphoreType.DMA((ntm - 1,)),
        ],
        compiler_params=pltpu.CompilerParams(
            collective_id=0, has_side_effects=True, vmem_limit_bytes=60 * 1024 * 1024),
    )(clips, w_time, keep, ids, keep[None], ids[None], rate[None], gain[None], w_lat.T)


def main_kernel(rows, per, clips, prior, w, maps, features, acc, xbuf, sems):
    step = pl.program_id(0)
    nframe = clips.shape[0]
    npos, nchan = clips.shape[1:]
    halo = KT - 1

    def load(slot):
        source = prior.at[slot] if slot < halo else clips.at[slot - halo]
        return pltpu.make_async_copy(source, xbuf.at[slot], sems.at[slot])

    @pl.when(step == 0)
    def _():
        for slot in range(nframe + halo):
            load(slot).start()
        for slot in range(halo):
            load(slot).wait()
        acc[...] = jnp.zeros_like(acc)

    first = step * per
    for k in range(per):
        at = first + k
        pltpu.make_async_copy(clips.at[at], xbuf.at[at + halo], sems.at[at + halo]).wait()

    def conv(at):
        span = pl.ds(at, rows)
        taps = [xbuf[pl.ds(first + halo - k, per), span].reshape(per * rows, nchan) for k in range(KT)]
        return taps[0], jnp.dot(jnp.concatenate(taps, axis=1), w[...], preferred_element_type=jnp.float32)

    def post(at, own, total):
        span = pl.ds(at, rows)
        half = 0.5 * total
        value = own.astype(jnp.float32) + (half * jnp.tanh(half) + half)
        rounded = value.astype(jnp.bfloat16)
        features[:, span] = rounded.reshape(per, rows, nchan)
        scale = lax.rsqrt(jnp.mean(value * value, axis=-1, keepdims=True) + 1e-06)
        out = acc[span]
        for k in range(per):
            part = slice(k * rows, (k + 1) * rows)
            out = out + scale[part] * jnp.dot(rounded[part], maps[k], preferred_element_type=jnp.float32)
        acc[span] = out

    held = None
    for at in range(0, npos, rows):
        now = conv(at)
        if held is not None:
            post(*held)
        held = (at, *now)
    post(*held)


def main_call(clips, prior, w, maps, rows=512, per=2):
    nframe, npos, nchan = clips.shape
    ncol = maps.shape[-1]
    halo = KT - 1
    return pl.pallas_call(
        functools.partial(main_kernel, rows, per),
        grid=(nframe // per,),
        out_shape=(
            jax.ShapeDtypeStruct((nframe, npos, nchan), jnp.bfloat16),
            jax.ShapeDtypeStruct((npos, ncol), jnp.float32),
        ),
        in_specs=[
            pl.BlockSpec(memory_space=pl.ANY),
            pl.BlockSpec(memory_space=pl.ANY),
            pl.BlockSpec(w.shape, lambda i: (0, 0)),
            pl.BlockSpec((per, nchan, ncol), lambda i: (i, 0, 0)),
        ],
        out_specs=(
            pl.BlockSpec((per, npos, nchan), lambda i: (i, 0, 0)),
            pl.BlockSpec((npos, ncol), lambda i: (0, 0)),
        ),
        scratch_shapes=[
            pltpu.VMEM((nframe + halo, npos, nchan), jnp.bfloat16),
            pltpu.SemaphoreType.DMA((nframe + halo,)),
        ],
        compiler_params=pltpu.CompilerParams(vmem_limit_bytes=56 * 1024 * 1024),
    )(clips, prior, w, maps)


def reduce_kernel(nchip, per, acc, out, mine, theirs, sums, slots, s1, r1, s2, r2):
    d, t = lax.axis_index("dp"), lax.axis_index("tm")
    c = lax.rem(t, 2)
    z = lax.div(t, 2)
    sister = t + 1 - 2 * c
    barrier = pltpu.get_barrier_semaphore()
    pl.semaphore_signal(barrier, inc=1, device_id=(d, sister), device_id_type=MESH)
    for k in range(1, nchip):
        pl.semaphore_signal(barrier, inc=1, device_id=(d, lax.rem(z + k, nchip) * 2 + c), device_id_type=MESH)
    turned = acc[...].T
    for e in range(2 * nchip):
        mine[e % 2, e // 2] = turned[e * per:(e + 1) * per]
    pl.semaphore_wait(barrier, nchip)
    swap = pltpu.make_async_remote_copy(
        src_ref=mine.at[1 - c], dst_ref=theirs, send_sem=s1, recv_sem=r1,
        device_id=(d, sister), device_id_type=MESH)
    swap.start()
    swap.wait_recv()
    sums[...] = (mine[c] + theirs[...]).astype(jnp.bfloat16)

    def copy(k):
        ahead = lax.rem(z + k, nchip)
        return pltpu.make_async_remote_copy(
            src_ref=sums.at[ahead], dst_ref=slots.at[k - 1], send_sem=s2.at[k - 1], recv_sem=r2.at[k - 1],
            device_id=(d, ahead * 2 + c), device_id_type=MESH)

    for k in range(nchip - 1, 0, -1):
        @pl.when(z + k < nchip)
        def _():
            copy(k).start()
    out[...] = mine[c, z] + theirs[z]
    for k in range(1, nchip):
        @pl.when(z >= k)
        def _():
            copy(k).wait_recv()
            out[...] += slots[k - 1].astype(jnp.float32)
    for k in range(1, nchip):
        @pl.when(z + k < nchip)
        def _():
            copy(k).wait_send()
    swap.wait_send()


def reduce_call(acc, per):
    npos, ncol = acc.shape
    nchip = lax.axis_size("tm") // 2
    vmem = pl.BlockSpec(memory_space=pltpu.VMEM)
    return pl.pallas_call(
        functools.partial(reduce_kernel, nchip, per),
        out_shape=jax.ShapeDtypeStruct((per, npos), jnp.float32),
        in_specs=[vmem],
        out_specs=vmem,
        scratch_shapes=[
            pltpu.VMEM((2, nchip, per, npos), jnp.float32),
            pltpu.VMEM((nchip, per, npos), jnp.float32),
            pltpu.VMEM((nchip, per, npos), jnp.bfloat16),
            pltpu.VMEM((nchip - 1, per, npos), jnp.bfloat16),
            pltpu.SemaphoreType.DMA,
            pltpu.SemaphoreType.DMA,
            pltpu.SemaphoreType.DMA((nchip - 1,)),
            pltpu.SemaphoreType.DMA((nchip - 1,)),
        ],
        compiler_params=pltpu.CompilerParams(
            collective_id=1, has_side_effects=True, vmem_limit_bytes=48 * 1024 * 1024),
    )(acc)


def per_device(clips, w_time, gain, rate, keep, latent_ids, w_lat):
    nclip, nframe, npos, nchan = clips.shape
    nown = nframe // STRIDE
    latc = w_lat.shape[1]
    w, prior, maps = gather_call(clips[0], w_time, gain, rate, keep, latent_ids, w_lat)
    features, acc = main_call(clips[0], prior, w.reshape(KT * nchan, nchan), maps)
    latents = reduce_call(acc, nown * latc).reshape(nown, latc, npos)
    return (features[None], latents[None])


def solution(mesh):
    return jax.shard_map(
        per_device,
        mesh=mesh,
        in_specs=(P("dp", "tm", None, None), P(None, "dp", None), P(), P(), P("tm"), P("tm"), P()),
        out_specs=(P("dp", "tm", None, None), P("dp", "tm", None, None)),
        check_vma=False,
    )
```

```python
import functools
import jax
import jax.numpy as jnp
from jax import lax
from jax.experimental import pallas as pl
from jax.experimental.pallas import tpu as pltpu
from jax.sharding import PartitionSpec as P

KT = 3
STRIDE = 8
NT = (((1,), (1,)), ((), ()))
HI = lax.Precision.HIGHEST


MESH = pl.DeviceIdType.MESH


def maps_of(nframe, nlat, base, keep_row, ids_row, keep_own, ids_own, rate_row, gain_row, w_lat, maps_ref):
    nall = keep_row.shape[1]
    latc, nchan = w_lat.shape
    ncol = nlat * latc
    rate_col = jnp.broadcast_to(rate_row, (128, nchan)).T[:, :1]
    gain_col = jnp.broadcast_to(gain_row, (128, nchan)).T[:, :1]
    spread = lax.broadcasted_iota(jnp.int32, (latc, ncol), 1) % latc == lax.broadcasted_iota(jnp.int32, (latc, ncol), 0)
    wl = lax.dot_general(w_lat, spread.astype(jnp.bfloat16), (((0,), (0,)), ((), ())), preferred_element_type=jnp.float32)
    end = base + nframe - 1
    frame = lax.broadcasted_iota(jnp.int32, (8, nall), 1)
    later = frame > end
    logs = jnp.where(later, jnp.log(keep_row), 0.0)
    tri = (lax.broadcasted_iota(jnp.int32, (nall, nall), 0) <= lax.broadcasted_iota(jnp.int32, (nall, nall), 1)).astype(jnp.float32)
    cum = jnp.dot(logs, tri, precision=HI, preferred_element_type=jnp.float32)[:1]
    steps = (frame[:1] - end).astype(jnp.float32)
    power = jnp.where(later[:1], cum - rate_col * steps, -200.0)
    dec = jnp.exp(power)
    pooled = (lax.broadcasted_iota(jnp.int32, (ncol, nall), 0) // latc == ids_row).astype(jnp.float32)
    entry = lax.dot_general(dec, pooled, NT, precision=HI, preferred_element_type=jnp.float32)
    counts = lax.dot_general(jnp.ones((8, nall), jnp.float32), pooled, NT, preferred_element_type=jnp.float32)[:1]
    inject = jnp.sqrt(1.0 - jnp.exp(-2.0 * rate_col))
    small = 2.0 * rate_col
    series = small * (1.0 - small * (0.5 - small * (1.0 / 6.0 - small * (1.0 / 24.0 - small * (1.0 / 120.0)))))
    inject = jnp.where(small < 0.125, jnp.sqrt(series), inject)
    weight = wl * (inject * gain_col) / counts
    decay = jnp.exp(-rate_col)
    column = lax.broadcasted_iota(jnp.int32, (1, ncol), 1) // latc
    here = [(column == ids_own(g)).astype(jnp.float32) for g in range(nframe)]
    yield
    chunk = nchan // 4
    for at in range(0, nchan, chunk):
        span = slice(at, at + chunk)
        scale, fade = weight[span], decay[span]
        total = here[nframe - 1] + entry[span]
        maps_ref[nframe - 1, span] = (scale * total).astype(jnp.bfloat16)
        for g in range(nframe - 2, -1, -1):
            total = here[g] + (fade * keep_own(g + 1)) * total
            maps_ref[g, span] = (scale * total).astype(jnp.bfloat16)
        yield


def gather_kernel(ntm, nlat, clips, w_time, keep_s, ids_s, keep_v, ids_v, rate, gain, w_lat,
                  w_full, prior, maps_out, maps, small, zeros, local_sem, map_sem, sw, rw, st, rt, sk, rk):
    halo = KT - 1
    nframe = clips.shape[0]
    shard = w_time.shape[1]
    d, t = lax.axis_index("dp"), lax.axis_index("tm")
    c = lax.rem(t, 2)
    sister = t + 1 - 2 * c
    xd = d + 1 - 2 * lax.rem(d, 2)
    yd = lax.rem(d + 2, 4)
    part = shard // 4

    barrier = pltpu.get_barrier_semaphore()
    for k in range(1, ntm):
        pl.semaphore_signal(barrier, inc=1, device_id=(d, lax.rem(t + k, ntm)), device_id_type=MESH)
    for other in (xd, yd):
        pl.semaphore_signal(barrier, inc=1, device_id=(other, t), device_id_type=MESH)
    own_copy = pltpu.make_async_copy(w_time, w_full.at[:, pl.ds(d * shard, shard)], local_sem.at[0])
    own_copy.start()
    nall = small.shape[-1]
    place = lax.broadcasted_iota(jnp.int32, (nframe, nall), 1) == lax.broadcasted_iota(jnp.int32, (nframe, nall), 0) + t * nframe
    place = place.astype(jnp.float32)
    keep8 = jnp.broadcast_to(keep_v[...], (8, nframe))
    ids8 = jnp.broadcast_to(ids_v[...].astype(jnp.float32), (8, nframe))
    pick = lax.broadcasted_iota(jnp.int32, (8, nframe), 0) == 0
    both = jnp.where(pick, keep8, ids8)
    small[0] = jnp.dot(both, place, precision=HI, preferred_element_type=jnp.float32)
    pl.semaphore_wait(barrier, ntm + 1)

    def rows(dev, core, q):
        return pl.ds(dev * shard + core * (2 * part) + q * part, part)

    def send(source, dest, index, device):
        return pltpu.make_async_remote_copy(
            src_ref=source, dst_ref=dest, send_sem=sw.at[index], recv_sem=rw.at[index],
            device_id=device, device_id_type=MESH)

    smalls = []
    for k in range(1, ntm):
        copy = pltpu.make_async_remote_copy(
            src_ref=small.at[0], dst_ref=small.at[k], send_sem=sk.at[k - 1], recv_sem=rk.at[k - 1],
            device_id=(d, lax.rem(t + k, ntm)), device_id_type=MESH)
        copy.start()
        smalls.append(copy)

    own = {}
    for q in range(2):
        source = w_time.at[:, pl.ds(c * (2 * part) + q * part, part)]
        dest = w_full.at[:, rows(d, c, q)]
        own[q] = send(source, dest, q, (xd, t))
        own[2 + q] = send(source, dest, 2 + q, (yd, t))
    for index in (0, 3, 1, 2):
        own[index].start()
    tail = pltpu.make_async_remote_copy(
        src_ref=clips.at[pl.ds(nframe - halo, halo)], dst_ref=prior, send_sem=st, recv_sem=rt,
        device_id=(d, lax.rem(t + 1, ntm)), device_id_type=MESH)

    @pl.when(t < ntm - 1)
    def _():
        tail.start()

    @pl.when(t == 0)
    def _():
        zeros[...] = jnp.zeros_like(zeros)
        for h in range(halo):
            pltpu.make_async_copy(zeros, prior.at[h], local_sem.at[1 + h]).start()

    diag = 3 - d
    got = {}
    def forward(dev, q, index, device):
        piece = w_full.at[:, rows(dev, c, q)]
        copy = send(piece, piece, index, device)
        copy.start()
        got[index] = copy

    own[0].wait_recv()
    forward(xd, 0, 4, (yd, t))
    forward(xd, 0, 6, (d, sister))
    own[3].wait_recv()
    forward(yd, 1, 5, (xd, t))
    forward(yd, 1, 9, (d, sister))
    own[1].wait_recv()
    forward(xd, 1, 7, (d, sister))
    own[2].wait_recv()
    forward(yd, 0, 8, (d, sister))

    for copy in smalls:
        copy.wait_recv()
    table = small[0]
    for k in range(1, ntm):
        table = table + small[k]

    making = maps_of(nframe, nlat, t * nframe, table[0:1], table[1:2].astype(jnp.int32),
                     lambda g: keep_s[g], lambda g: ids_s[g], rate[...], gain[...], w_lat[...], maps)
    next(making)
    got[4].wait_recv()
    forward(diag, 0, 10, (d, sister))
    got[5].wait_recv()
    forward(diag, 1, 11, (d, sister))
    chunk = maps.shape[1] // 4
    leaving = []
    for k in range(4):
        next(making)
        span = pl.ds(k * chunk, chunk)
        copy = pltpu.make_async_copy(maps.at[:, span], maps_out.at[:, span], map_sem.at[k])
        copy.start()
        leaving.append(copy)
    for index in range(6, 12):
        got[index].wait_recv()
    for index in range(4):
        own[index].wait_send()
    for index in range(4, 12):
        got[index].wait_send()
    for copy in smalls:
        copy.wait_send()
    own_copy.wait()
    for copy in leaving:
        copy.wait()

    @pl.when(t == 0)
    def _():
        for h in range(halo):
            pltpu.make_async_copy(zeros, prior.at[h], local_sem.at[1 + h]).wait()

    @pl.when(t < ntm - 1)
    def _():
        tail.wait_send()

    @pl.when(t > 0)
    def _():
        tail.wait_recv()


def gather_call(clips, w_time, gain, rate, keep, ids, w_lat):
    nframe, npos, nchan = clips.shape
    ntm = lax.axis_size("tm")
    nall = nframe * ntm
    nlat = nall // STRIDE
    ncol = nlat * w_lat.shape[1]
    any_spec = pl.BlockSpec(memory_space=pl.ANY)
    smem = pl.BlockSpec(memory_space=pltpu.SMEM)
    vmem = pl.BlockSpec(memory_space=pltpu.VMEM)
    return pl.pallas_call(
        functools.partial(gather_kernel, ntm, nlat),
        out_shape=(
            jax.ShapeDtypeStruct((KT, nchan, nchan), jnp.bfloat16),
            jax.ShapeDtypeStruct((KT - 1, npos, nchan), jnp.bfloat16),
            jax.ShapeDtypeStruct((nframe, nchan, ncol), jnp.bfloat16),
        ),
        in_specs=[any_spec, any_spec, smem, smem] + [vmem] * 5,
        out_specs=(any_spec, any_spec, any_spec),
        scratch_shapes=[
            pltpu.VMEM((nframe, nchan, ncol), jnp.bfloat16),
            pltpu.VMEM((ntm, 8, nall), jnp.float32),
            pltpu.VMEM((npos, nchan), jnp.bfloat16),
            pltpu.SemaphoreType.DMA((KT,)),
            pltpu.SemaphoreType.DMA((4,)),
            pltpu.SemaphoreType.DMA((12,)),
            pltpu.SemaphoreType.DMA((12,)),
            pltpu.SemaphoreType.DMA,
            pltpu.SemaphoreType.DMA,
            pltpu.SemaphoreType.DMA((ntm - 1,)),
            pltpu.SemaphoreType.DMA((ntm - 1,)),
        ],
        compiler_params=pltpu.CompilerParams(
            collective_id=0, has_side_effects=True, vmem_limit_bytes=60 * 1024 * 1024),
    )(clips, w_time, keep, ids, keep[None], ids[None], rate[None], gain[None], w_lat.T)


def main_kernel(rows, per, clips, prior, w, maps, features, acc, xbuf, sems):
    step = pl.program_id(0)
    nframe = clips.shape[0]
    npos, nchan = clips.shape[1:]
    halo = KT - 1

    def load(slot):
        source = prior.at[slot] if slot < halo else clips.at[slot - halo]
        return pltpu.make_async_copy(source, xbuf.at[slot], sems.at[slot])

    @pl.when(step == 0)
    def _():
        for slot in range(nframe + halo):
            load(slot).start()
        for slot in range(halo):
            load(slot).wait()
        acc[...] = jnp.zeros_like(acc)

    first = step * per
    for k in range(per):
        at = first + k
        pltpu.make_async_copy(clips.at[at], xbuf.at[at + halo], sems.at[at + halo]).wait()

    def conv(at):
        span = pl.ds(at, rows)
        taps = [xbuf[pl.ds(first + halo - k, per), span].reshape(per * rows, nchan) for k in range(KT)]
        return taps[0], jnp.dot(jnp.concatenate(taps, axis=1), w[...], preferred_element_type=jnp.float32)

    def post(at, own, total):
        span = pl.ds(at, rows)
        half = 0.5 * total
        value = own.astype(jnp.float32) + (half * jnp.tanh(half) + half)
        rounded = value.astype(jnp.bfloat16)
        features[:, span] = rounded.reshape(per, rows, nchan)
        scale = lax.rsqrt(jnp.mean(value * value, axis=-1, keepdims=True) + 1e-06)
        out = acc[span]
        for k in range(per):
            part = slice(k * rows, (k + 1) * rows)
            out = out + scale[part] * jnp.dot(rounded[part], maps[k], preferred_element_type=jnp.float32)
        acc[span] = out

    held = None
    for at in range(0, npos, rows):
        now = conv(at)
        if held is not None:
            post(*held)
        held = (at, *now)
    post(*held)


def main_call(clips, prior, w, maps, rows=512, per=2):
    nframe, npos, nchan = clips.shape
    ncol = maps.shape[-1]
    halo = KT - 1
    return pl.pallas_call(
        functools.partial(main_kernel, rows, per),
        grid=(nframe // per,),
        out_shape=(
            jax.ShapeDtypeStruct((nframe, npos, nchan), jnp.bfloat16),
            jax.ShapeDtypeStruct((npos, ncol), jnp.float32),
        ),
        in_specs=[
            pl.BlockSpec(memory_space=pl.ANY),
            pl.BlockSpec(memory_space=pl.ANY),
            pl.BlockSpec(w.shape, lambda i: (0, 0)),
            pl.BlockSpec((per, nchan, ncol), lambda i: (i, 0, 0)),
        ],
        out_specs=(
            pl.BlockSpec((per, npos, nchan), lambda i: (i, 0, 0)),
            pl.BlockSpec((npos, ncol), lambda i: (0, 0)),
        ),
        scratch_shapes=[
            pltpu.VMEM((nframe + halo, npos, nchan), jnp.bfloat16),
            pltpu.SemaphoreType.DMA((nframe + halo,)),
        ],
        compiler_params=pltpu.CompilerParams(vmem_limit_bytes=56 * 1024 * 1024),
    )(clips, prior, w, maps)


def reduce_kernel(nchip, per, acc, out, mine, theirs, sums, slots, s1, r1, s2, r2):
    d, t = lax.axis_index("dp"), lax.axis_index("tm")
    c = lax.rem(t, 2)
    z = lax.div(t, 2)
    sister = t + 1 - 2 * c
    barrier = pltpu.get_barrier_semaphore()
    pl.semaphore_signal(barrier, inc=1, device_id=(d, sister), device_id_type=MESH)
    for k in range(1, nchip):
        pl.semaphore_signal(barrier, inc=1, device_id=(d, lax.rem(z + k, nchip) * 2 + c), device_id_type=MESH)
    turned = acc[...].T
    for e in range(2 * nchip):
        mine[e % 2, e // 2] = turned[e * per:(e + 1) * per]
    pl.semaphore_wait(barrier, nchip)
    swap = pltpu.make_async_remote_copy(
        src_ref=mine.at[1 - c], dst_ref=theirs, send_sem=s1, recv_sem=r1,
        device_id=(d, sister), device_id_type=MESH)
    swap.start()
    swap.wait_recv()
    sums[...] = (mine[c] + theirs[...]).astype(jnp.bfloat16)

    def copy(k):
        ahead = lax.rem(z + k, nchip)
        return pltpu.make_async_remote_copy(
            src_ref=sums.at[ahead], dst_ref=slots.at[k - 1], send_sem=s2.at[k - 1], recv_sem=r2.at[k - 1],
            device_id=(d, ahead * 2 + c), device_id_type=MESH)

    for k in range(nchip - 1, 0, -1):
        @pl.when(z + k < nchip)
        def _():
            copy(k).start()
    out[...] = mine[c, z] + theirs[z]
    for k in range(1, nchip):
        @pl.when(z >= k)
        def _():
            copy(k).wait_recv()
            out[...] += slots[k - 1].astype(jnp.float32)
    for k in range(1, nchip):
        @pl.when(z + k < nchip)
        def _():
            copy(k).wait_send()
    swap.wait_send()


def reduce_call(acc, per):
    npos, ncol = acc.shape
    nchip = lax.axis_size("tm") // 2
    vmem = pl.BlockSpec(memory_space=pltpu.VMEM)
    return pl.pallas_call(
        functools.partial(reduce_kernel, nchip, per),
        out_shape=jax.ShapeDtypeStruct((per, npos), jnp.float32),
        in_specs=[vmem],
        out_specs=vmem,
        scratch_shapes=[
            pltpu.VMEM((2, nchip, per, npos), jnp.float32),
            pltpu.VMEM((nchip, per, npos), jnp.float32),
            pltpu.VMEM((nchip, per, npos), jnp.bfloat16),
            pltpu.VMEM((nchip - 1, per, npos), jnp.bfloat16),
            pltpu.SemaphoreType.DMA,
            pltpu.SemaphoreType.DMA,
            pltpu.SemaphoreType.DMA((nchip - 1,)),
            pltpu.SemaphoreType.DMA((nchip - 1,)),
        ],
        compiler_params=pltpu.CompilerParams(
            collective_id=1, has_side_effects=True, vmem_limit_bytes=48 * 1024 * 1024),
    )(acc)


def per_device(clips, w_time, gain, rate, keep, latent_ids, w_lat):
    nclip, nframe, npos, nchan = clips.shape
    nown = nframe // STRIDE
    latc = w_lat.shape[1]
    w, prior, maps = gather_call(clips[0], w_time, gain, rate, keep, latent_ids, w_lat)
    features, acc = main_call(clips[0], prior, w.reshape(KT * nchan, nchan), maps)
    latents = reduce_call(acc, nown * latc).reshape(nown, latc, npos)
    return (features[None], latents[None])


def solution(mesh):
    return jax.shard_map(
        per_device,
        mesh=mesh,
        in_specs=(P("dp", "tm", None, None), P(None, "dp", None), P(), P(), P("tm"), P("tm"), P()),
        out_specs=(P("dp", "tm", None, None), P("dp", "tm", None, None)),
        check_vma=False,
    )
```
